256 devices in a mesh: dom: 16 (over z, core), orb: 16 (over y, x).
Axes of the slice: x: 4, y: 4, z: 8, core: 2. Of those that a mesh axis runs over, the one named last changes fastest.
Arguments:
- green_blocks: bfloat16 [16, 2048, 2048], P('dom', 'orb'), may hold values from -2 to 2
- couplings: bfloat16 [16, 2048, 2048], P('dom', 'orb'), may hold values from -0.125 to 0.125
- pattern: int32 [16, 32, 32], P('dom', 'orb'), may hold values 0 or 1
- sources: bfloat16 [16, 64, 2048], P('dom', None, 'orb'), may hold values from -6 to 6
- injected: bfloat16 [64, 2048], replicated, may hold values from -6 to 6
Outputs:
- states: bfloat16 [16, 64, 2048], P('dom', None, 'orb')
The draws below stay inside these ranges and needn't reach their ends.
All inputs are finite; a program needn't handle non-finite values. No bound on the sum of `pattern` on one device may be relied on, other than what follows from the above.
Results may differ from the reference program's by a relative error of at most 0.025.
Values may be sent and summed in bfloat16 or wider, within the bound.
No kernel may reach another device: no remote copies, remote signals or barrier semaphores. Data moves between devices by JAX's collectives and lax.ppermute only.
A program may use at most 64 MiB of HBM per device.

```python
import jax
import jax.numpy as jnp
from jax import lax

M = 2048
BLOCK = 64
MODES = 64
SLABS = 16
BLOCKS = 32


def draw_green_blocks(key, part):
    key = jax.random.fold_in(key, 11)
    first_key, second_key = jax.random.split(key)
    shape = (SLABS, M, M)
    noise = jax.random.truncated_normal(first_key, -4.0, 4.0, shape, jnp.float32) * 0.3
    diagonal = jnp.exp(jax.random.uniform(second_key, (SLABS, M), jnp.float32, 0.0, 0.4))
    identity = (lax.broadcasted_iota(jnp.int32, (M, M), 0) == lax.broadcasted_iota(jnp.int32, (M, M), 1)).astype(jnp.float32)
    return (noise / M ** 0.5 + diagonal[:, :, None] * identity[None]).astype(jnp.bfloat16)


def with_ends(values, rng, least, top_value):
    dims = values.shape
    index_at = [jax.random.randint(jax.random.fold_in(rng, axis), (), 0, dims[axis]) for axis in range(len(dims))]
    values = values.at[tuple(index_at)].set(least)
    longest = dims.index(max(dims))
    index_at[longest] = (index_at[longest] + 1) % dims[longest]
    return values.at[tuple(index_at)].set(top_value)


def level_of(own_key, dims, cuts, least, top_value):
    factor_of = 1.0
    for axis_at, blocks in cuts:
        steps = jax.random.uniform(jax.random.fold_in(jax.random.fold_in(own_key, 6), axis_at), (blocks,), jnp.float32, least / len(cuts), top_value / len(cuts))
        factor_of = factor_of * jnp.repeat(jnp.exp(steps), dims[axis_at] // blocks).reshape((-1,) + (1,) * (len(dims) - 1 - axis_at))
    return factor_of


def bell_draw(stream_key, extent, scale, bound, cuts=(), kind=jnp.bfloat16):
    values = jax.random.normal(stream_key, extent, jnp.float32) * scale
    if len(cuts) > 0:
        values = level_of(stream_key, extent, cuts, -0.22, 0.18) * values
    return jnp.clip(values, min=-bound, max=bound).astype(kind)


def setup_inputs(seed: int = 0) -> dict:
    streams_of = jax.random.split(jax.random.key(seed), 6)
    green_blocks = draw_green_blocks(jax.random.fold_in(streams_of[5], 71), 0)
    couplings = bell_draw(streams_of[1], (SLABS, M, M), M ** -0.5, 0.125, ((0, 16), (1, 16)))
    pattern = with_ends((jax.random.randint(streams_of[2], (SLABS, BLOCKS, BLOCKS), 0, 2) < 1).astype(jnp.int32), jax.random.fold_in(streams_of[2], 1), 0, 1)
    sources = bell_draw(streams_of[3], (SLABS, MODES, M), 1.0, 6.0, ((0, 16), (2, 16)))
    injected = bell_draw(streams_of[4], (MODES, M), 1.0, 6.0)
    return {"green_blocks": green_blocks, "couplings": couplings, "pattern": pattern, "sources": sources, "injected": injected}


def reference(green_blocks, couplings, pattern, sources, injected):
    def advance(previous, slab_items):
        green_rows, coupling, block_mask, source = slab_items
        expanded = jnp.repeat(jnp.repeat(block_mask, BLOCK, axis=0), BLOCK, axis=1).astype(coupling.dtype)
        masked = coupling * expanded
        transfer = jnp.dot(green_rows, masked, preferred_element_type=jnp.float32).astype(jnp.bfloat16)
        current = source.astype(jnp.float32) - jnp.dot(previous, transfer.T, preferred_element_type=jnp.float32)
        current = current.astype(jnp.bfloat16)
        return current, current

    _, states = lax.scan(advance, injected, (green_blocks, couplings, pattern, sources))
    return states
```

```python
import jax
import jax.numpy as jnp
from jax import lax
from jax.sharding import PartitionSpec as P

BLOCK = 64
SIDE = 4


def moved(value, dy, dx):
    pairs = [
        (SIDE * y + x, SIDE * ((y + dy) % SIDE) + (x + dx) % SIDE)
        for y in range(SIDE)
        for x in range(SIDE)
    ]
    return lax.ppermute(value, "orb", pairs)


def ring(value, along_x, place, index):
    up, down = ((0, 1), (0, -1)) if along_x else ((1, 0), (-1, 0))
    half = value.shape[0] // 2
    before = moved(value, *up)
    after = moved(value, *down)
    far_low = moved(before[:half], *up)
    far_high = moved(after[half:], *down)
    at = lambda offset: (index + offset) % SIDE
    place(at(0), 0, value)
    place(at(3), 0, before)
    place(at(1), 0, after)
    place(at(2), 0, far_low)
    place(at(2), half, far_high)


def gathered_rows(value, along_x, index):
    size = value.shape[0]
    buffer = jnp.zeros((SIDE * size, value.shape[1]), value.dtype)

    def place(turn, skip, piece):
        nonlocal buffer
        buffer = lax.dynamic_update_slice(buffer, piece, (turn * size + skip, 0))

    ring(value, along_x, place, index)
    return buffer


def gathered_columns(value, along_x, index):
    size = value.shape[1]
    buffer = jnp.zeros((value.shape[0], SIDE * size), value.dtype)

    def place(turn, skip, piece):
        nonlocal buffer
        buffer = lax.dynamic_update_slice(buffer, piece, (skip, turn * size))

    ring(value, along_x, place, index)
    return buffer


def on_device(green_blocks, couplings, pattern, sources, injected):
    orb = lax.axis_index("orb")
    dom = lax.axis_index("dom")
    y, x = orb // SIDE, orb % SIDE
    green = green_blocks[0]
    rows, order = green.shape
    wide = order // SIDE
    half = wide // 2
    expanded = jnp.repeat(jnp.repeat(pattern[0], BLOCK, axis=0), BLOCK, axis=1).astype(jnp.bfloat16)
    masked = couplings[0] * expanded

    def part(offset):
        turn = (x + offset) % SIDE
        low = lax.dynamic_slice_in_dim(masked, turn * half, half, 1)
        high = lax.dynamic_slice_in_dim(masked, order // 2 + turn * half, half, 1)
        return jnp.concatenate([low, high], axis=1)

    columns = jnp.zeros((SIDE * rows, wide), masked.dtype)
    for offset in range(SIDE):
        piece = moved(part(offset), 0, offset) if offset else part(0)
        columns = lax.dynamic_update_slice(columns, piece, ((x - offset) % SIDE * rows, 0))
    columns = gathered_rows(columns, False, y)
    green_rows = gathered_rows(green, True, x)

    tile = lax.dot_general(
        columns, green_rows, (((0,), (1,)), ((), ())), preferred_element_type=jnp.float32
    ).astype(jnp.bfloat16)

    low = gathered_columns(gathered_rows(tile[:half], True, x), False, y)
    high = gathered_rows(gathered_columns(tile[half:], False, y), True, x)

    low, high = lax.optimization_barrier((low, high))

    modes = injected.shape[0] // (SIDE * SIDE)
    source = lax.all_to_all(sources[0], "orb", 0, 1, tiled=True).astype(jnp.float32)
    incoming = lax.dynamic_slice_in_dim(injected, orb * modes, modes, 0)
    slabs = lax.axis_size("dom")
    for slab in range(slabs):
        product = jnp.dot(incoming[:, : order // 2], low, preferred_element_type=jnp.float32)
        product += jnp.dot(incoming[:, order // 2 :], high, preferred_element_type=jnp.float32)
        current = (source - product).astype(jnp.bfloat16)
        if slab + 1 < slabs:
            passed = lax.ppermute(current, "dom", [(slab, slab + 1)])
            incoming = jnp.where(dom == slab + 1, passed, incoming)
    return lax.all_to_all(current, "orb", 1, 0, tiled=True)[None]


def solution(mesh):
    return jax.shard_map(
        on_device,
        mesh=mesh,
        in_specs=(
            P("dom", "orb", None),
            P("dom", "orb", None),
            P("dom", "orb", None),
            P("dom", None, "orb"),
            P(),
        ),
        out_specs=P("dom", None, "orb"),
        check_vma=False,
    )
```

```python
import jax
import jax.numpy as jnp
from jax import lax
from jax.experimental import pallas as pl
from jax.experimental.pallas import tpu as pltpu
from jax.sharding import PartitionSpec as P

BLOCK = 64
SIDE = 4


def moved(value, dy, dx):
    pairs = [
        (SIDE * y + x, SIDE * ((y + dy) % SIDE) + (x + dx) % SIDE)
        for y in range(SIDE)
        for x in range(SIDE)
    ]
    return lax.ppermute(value, "orb", pairs)


def ring(value, along_x, place, index):
    up, down = ((0, 1), (0, -1)) if along_x else ((1, 0), (-1, 0))
    half = value.shape[0] // 2
    before = moved(value, *up)
    after = moved(value, *down)
    far_low = moved(before[:half], *up)
    far_high = moved(after[half:], *down)
    at = lambda offset: (index + offset) % SIDE
    place(at(0), 0, value)
    place(at(3), 0, before)
    place(at(1), 0, after)
    place(at(2), 0, far_low)
    place(at(2), half, far_high)


def gathered_rows(value, along_x, index):
    size = value.shape[0]
    buffer = jnp.zeros((SIDE * size, value.shape[1]), value.dtype)

    def place(turn, skip, piece):
        nonlocal buffer
        buffer = lax.dynamic_update_slice(buffer, piece, (turn * size + skip, 0))

    ring(value, along_x, place, index)
    return buffer


def gathered_columns(value, along_x, index):
    size = value.shape[1]
    buffer = jnp.zeros((value.shape[0], SIDE * size), value.dtype)

    def place(turn, skip, piece):
        nonlocal buffer
        buffer = lax.dynamic_update_slice(buffer, piece, (skip, turn * size))

    ring(value, along_x, place, index)
    return buffer


def advance_kernel(passed, incoming, source, low, high, current, kept):
    state = passed[...] + incoming[...]
    kept[...] = state
    depth = low.shape[0]
    product = jnp.dot(state[:, :depth], low[...], preferred_element_type=jnp.float32)
    product += jnp.dot(state[:, depth:], high[...], preferred_element_type=jnp.float32)
    current[...] = (source[...].astype(jnp.float32) - product).astype(jnp.bfloat16)


def advanced(passed, incoming, source, low, high):
    near = lambda value: pltpu.with_memory_space_constraint(value, pltpu.VMEM)
    whole = pl.BlockSpec(memory_space=pltpu.VMEM)
    like = jax.ShapeDtypeStruct(passed.shape, passed.dtype)
    return pl.pallas_call(
        advance_kernel,
        out_shape=[like, like],
        in_specs=[whole] * 5,
        out_specs=[whole] * 2,
        compiler_params=pltpu.CompilerParams(vmem_limit_bytes=24 << 20),
        cost_estimate=pl.CostEstimate(flops=2 * 8 * low.size * 2, bytes_accessed=2 * 4 * low.size, transcendentals=0),
    )(passed, incoming, source, near(low), near(high))


def on_device(green_blocks, couplings, pattern, sources, injected):
    orb = lax.axis_index("orb")
    dom = lax.axis_index("dom")
    y, x = orb // SIDE, orb % SIDE
    green = green_blocks[0]
    rows, order = green.shape
    wide = order // SIDE
    half = wide // 2
    expanded = jnp.repeat(jnp.repeat(pattern[0], BLOCK, axis=0), BLOCK, axis=1).astype(jnp.bfloat16)
    masked = couplings[0] * expanded

    def part(offset):
        turn = (x + offset) % SIDE
        low = lax.dynamic_slice_in_dim(masked, turn * half, half, 1)
        high = lax.dynamic_slice_in_dim(masked, order // 2 + turn * half, half, 1)
        return jnp.concatenate([low, high], axis=1)

    columns = jnp.zeros((SIDE * rows, wide), masked.dtype)
    for offset in range(SIDE):
        piece = moved(part(offset), 0, offset) if offset else part(0)
        columns = lax.dynamic_update_slice(columns, piece, ((x - offset) % SIDE * rows, 0))
    columns = gathered_rows(columns, False, y)
    green_rows = gathered_rows(green, True, x)

    tile = lax.dot_general(
        columns, green_rows, (((0,), (1,)), ((), ())), preferred_element_type=jnp.float32
    ).astype(jnp.bfloat16)

    low = gathered_columns(gathered_rows(tile[:half], True, x), False, y)
    high = gathered_rows(gathered_columns(tile[half:], False, y), True, x)

    modes = injected.shape[0] // (SIDE * SIDE)
    source = lax.all_to_all(sources[0], "orb", 0, 1, tiled=True)
    start = lax.dynamic_slice_in_dim(injected, orb * modes, modes, 0)
    incoming = jnp.where(dom == 0, start, jnp.zeros_like(start))
    passed = jnp.zeros_like(start)
    slabs = lax.axis_size("dom")
    for slab in range(slabs):
        current, incoming = advanced(passed, incoming, source, low, high)
        if slab + 1 < slabs:
            passed = lax.ppermute(current, "dom", [(slab, slab + 1)])
    return lax.all_to_all(current, "orb", 1, 0, tiled=True)[None]


def solution(mesh):
    return jax.shard_map(
        on_device,
        mesh=mesh,
        in_specs=(
            P("dom", "orb", None),
            P("dom", "orb", None),
            P("dom", "orb", None),
            P("dom", None, "orb"),
            P(),
        ),
        out_specs=P("dom", None, "orb"),
        check_vma=False,
    )
```

```python
import functools

import jax
import jax.numpy as jnp
from jax import lax
from jax.experimental import pallas as pl
from jax.experimental.pallas import tpu as pltpu
from jax.sharding import PartitionSpec as P

BLOCK = 64
SIDE = 4
CORES = 2
OFFSETS = (0, -1, 1, 2)
WHOLE = pl.BlockSpec(memory_space=pltpu.VMEM)
SCALARS = pl.BlockSpec(memory_space=pltpu.SMEM)


def near(value):
    return pltpu.with_memory_space_constraint(value, pltpu.VMEM)


def bf16(*shape):
    return jax.ShapeDtypeStruct(shape, jnp.bfloat16)


def sent(value, planes, target):
    pairs = []
    for z in range(planes):
        for k in range(CORES):
            for y in range(SIDE):
                for x in range(SIDE):
                    to = target(z, k, y, x)
                    if to is not None:
                        number = lambda z, k, y, x: ((z * CORES + k) * SIDE + y % SIDE) * SIDE + x % SIDE
                        pairs.append((number(z, k, y, x), number(*to)))
    return lax.ppermute(value, ("dom", "orb"), pairs)


def ring(low, high, move):
    low_before, high_after = move(low, 1), move(high, -1)
    high_before, low_after = move(high, 1), move(low, -1)
    low_far, high_far = move(low_before, 1), move(high_after, -1)
    return [(low, high), (low_before, high_before), (low_after, high_after), (low_far, high_far)]


def mask_kernel(info, coupling, pattern, *refs):
    pieces, (masked, done) = refs[:SIDE], refs[SIDE:]
    rows, order = coupling.shape
    fetch = pltpu.make_async_copy(coupling, masked, done)
    fetch.start()
    blocks = order // BLOCK
    column_block = lax.broadcasted_iota(jnp.int32, (blocks, order), 1) // BLOCK
    spread = (column_block == lax.broadcasted_iota(jnp.int32, (blocks, order), 0)).astype(jnp.bfloat16)
    present = jnp.dot(pattern[...].astype(jnp.bfloat16), spread, preferred_element_type=jnp.float32)
    fetch.wait()
    for at in range(rows // BLOCK):
        part = slice(at * BLOCK, (at + 1) * BLOCK)
        masked[part, :] = masked[part, :] * present[at : at + 1, :].astype(jnp.bfloat16)
    wide = order // SIDE
    for offset in range(SIDE):
        turn = lax.rem(info[2] + offset, SIDE)
        pieces[offset][...] = masked[:, pl.ds(pl.multiple_of(turn * wide, wide), wide)]


def masked_pieces(info, coupling, pattern):
    rows, order = coupling.shape
    return pl.pallas_call(
        mask_kernel,
        out_shape=[pltpu.VMEM((rows, order // SIDE), jnp.bfloat16)] * SIDE,
        in_specs=[SCALARS, pl.BlockSpec(memory_space=pltpu.HBM), WHOLE],
        out_specs=[WHOLE] * SIDE,
        scratch_shapes=[pltpu.VMEM((rows, order), jnp.bfloat16), pltpu.SemaphoreType.DMA],
        compiler_params=pltpu.CompilerParams(vmem_limit_bytes=4 << 20),
    )(info, coupling, pattern)


def halves_kernel(green, after, low, high, done):
    half = low.shape[0]
    copies = [
        pltpu.make_async_copy(green.at[pl.ds(at * half, half)], out, done.at[at]) for at, out in enumerate((low, high))
    ]
    for copy in copies:
        copy.start()
    for copy in copies:
        copy.wait()


def halves(green, after):
    rows, order = green.shape
    return pl.pallas_call(
        halves_kernel,
        out_shape=[pltpu.VMEM((rows // 2, order), jnp.bfloat16)] * 2,
        in_specs=[pl.BlockSpec(memory_space=pltpu.HBM), pl.BlockSpec(memory_space=pl.ANY)],
        out_specs=[WHOLE] * 2,
        scratch_shapes=[pltpu.SemaphoreType.DMA((2,))],
        compiler_params=pltpu.CompilerParams(vmem_limit_bytes=2 << 20),
    )(green, after)


def tile_kernel(info, *refs):
    count = 2 * SIDE
    columns, greens = refs[:count], refs[count : 2 * count]
    out_low, out_high, all_columns, all_greens = refs[2 * count :]
    core, a, b = info[0], info[1], info[2]
    rows = columns[0].shape[0] // 2
    for at, offset in enumerate(OFFSETS):
        row_turn = lax.rem(a + (offset + SIDE), SIDE)
        green_turn = lax.rem(b + (offset + SIDE), SIDE)
        for half in range(2):
            for inner in range(2):
                turn = lax.rem(b + (SIDE - 2 * half - inner), SIDE)
                block = jnp.where(core == 0, SIDE * row_turn + turn, SIDE * turn + row_turn)
                place = pl.ds(pl.multiple_of(block * rows, rows), rows)
                all_columns[place, :] = columns[2 * at + half][inner * rows : (inner + 1) * rows, :]
            part = greens[2 * at + half]
            size = part.shape[0]
            start = pl.multiple_of((2 * green_turn + half) * size, size)
            all_greens[pl.ds(start, size), :] = part[...]
    tile = jnp.dot(all_greens[...], all_columns[...], preferred_element_type=jnp.float32)
    middle = tile.shape[1] // 2
    out_low[...] = tile[:, :middle].T.astype(jnp.bfloat16)
    out_high[...] = tile[:, middle:].T.astype(jnp.bfloat16)


def tiled(info, columns, greens):
    columns = [half for pair in columns for half in pair]
    greens = [half for pair in greens for half in pair]
    wide = columns[0].shape[1]
    order = greens[0].shape[1]
    return pl.pallas_call(
        tile_kernel,
        out_shape=[bf16(wide // 2, wide)] * 2,
        in_specs=[SCALARS] + [WHOLE] * 16,
        out_specs=[WHOLE] * 2,
        scratch_shapes=[pltpu.VMEM((order, wide), jnp.bfloat16), pltpu.VMEM((wide, order), jnp.bfloat16)],
        compiler_params=pltpu.CompilerParams(vmem_limit_bytes=12 << 20),
    )(info, *map(near, columns + greens))


def arrange_kernel(info, *refs):
    own, other, (even, odd) = refs[:8], refs[8:16], refs[16:]
    core, x = info[0], info[3]
    half, wide = own[0].shape
    block = wide // SIDE

    def arrange(from_even, from_odd):
        for at, offset in enumerate(OFFSETS):
            turn = lax.rem(x + (offset + SIDE), SIDE)
            for side in range(2):
                even[pl.ds(pl.multiple_of(turn * wide + side * half, half), half), :] = from_even[2 * at + side][...]
                for row in range(SIDE):
                    place = pl.ds(pl.multiple_of((SIDE * row + turn) * block, block), block)
                    piece = from_odd[2 * at + side][:, row * block : (row + 1) * block]
                    odd[side * half : (side + 1) * half, place] = piece

    pl.when(core == 0)(lambda: arrange(own, other))
    pl.when(core != 0)(lambda: arrange(other, own))


def arranged(info, own, other):
    wide = own[0].shape[1]
    order = SIDE * wide
    return pl.pallas_call(
        arrange_kernel,
        out_shape=[pltpu.VMEM((order, wide), jnp.bfloat16), pltpu.VMEM((wide, order), jnp.bfloat16)],
        in_specs=[SCALARS] + [WHOLE] * 16,
        out_specs=[WHOLE] * 2,
        compiler_params=pltpu.CompilerParams(vmem_limit_bytes=4 << 20),
    )(info, *map(near, own), *map(near, other))


def plane_kernel(at, info, state, *refs):
    arrived, refs = refs[:SIDE], refs[SIDE:]
    even_source, odd_source, even, odd, odd_part, even_state, kept = refs
    plane, y = info[5], info[4]
    wide = even_state.shape[1]
    total = arrived[0][...].astype(jnp.float32)
    for piece in arrived[1:]:
        total += piece[...].astype(jnp.float32)
    total = jnp.where(plane == at, total, 0.0) + state[...].astype(jnp.float32)
    total = total.astype(jnp.bfloat16)
    kept[...] = total
    product = jnp.dot(total, even[...], preferred_element_type=jnp.float32)
    current = (even_source[...].astype(jnp.float32) - product).astype(jnp.bfloat16)
    even_state[...] = current
    product = jnp.dot(current, odd[...], preferred_element_type=jnp.float32)
    odd_part[...] = (odd_source[...].astype(jnp.float32) - product).astype(jnp.bfloat16)


def through_plane(at, info, state, arrived, sources, even, odd):
    modes, order = state.shape
    wide = even.shape[1]
    return pl.pallas_call(
        functools.partial(plane_kernel, at),
        out_shape=[pltpu.VMEM((modes, columns), jnp.bfloat16) for columns in (order, wide, order)],
        in_specs=[SCALARS] + [WHOLE] * 9,
        out_specs=[WHOLE] * 3,
        compiler_params=pltpu.CompilerParams(vmem_limit_bytes=4 << 20),
    )(info, *map(near, (state, *arrived, *sources, even, odd)))


def on_device(green_blocks, couplings, pattern, sources, injected):
    orb, dom = lax.axis_index("orb"), lax.axis_index("dom")
    planes = lax.axis_size("dom") // CORES
    y, x = orb // SIDE, orb % SIDE
    plane, core = dom // CORES, dom % CORES
    first = core == 0
    a, b = jnp.where(first, y, x), jnp.where(first, x, y)
    info = jnp.stack([core, a, b, x, y, plane]).astype(jnp.int32)
    send = functools.partial(sent, planes=planes)
    along_x = lambda value, step: send(value, target=lambda z, k, y, x: (z, k, y, x + step))
    along_b = lambda value, step: send(value, target=lambda z, k, y, x: (z, k, y + k * step, x + (1 - k) * step))
    along_a = lambda value, step: send(value, target=lambda z, k, y, x: (z, k, y + (1 - k) * step, x + k * step))
    to_other_core = lambda value: send(value, target=lambda z, k, y, x: (z, 1 - k, y, x))

    pieces = masked_pieces(info, couplings[0], pattern[0])
    green_low, green_high = halves(green_blocks[0], pieces[0])
    pieces = [pieces[0]] + [along_b(pieces[offset], offset) for offset in range(1, SIDE)]
    greens = ring(green_low, green_high, along_b)
    columns = ring(jnp.concatenate(pieces[:2]), jnp.concatenate(pieces[2:]), along_a)
    tile_low, tile_high = tiled(info, columns, greens)
    own = [half for pair in ring(tile_low, tile_high, along_x) for half in pair]
    other = [to_other_core(half) for half in own]
    even, odd = arranged(info, own, other)

    order = injected.shape[1]
    wide = order // SIDE
    modes = injected.shape[0] // (SIDE * CORES)
    by_x = sources[0].reshape(SIDE, CORES * modes, -1)
    source = jnp.zeros((CORES * modes, wide), jnp.bfloat16)
    for step in range(SIDE):
        piece = lax.dynamic_index_in_dim(by_x, (x + step) % SIDE, 0, keepdims=False)
        piece = along_x(piece, step) if step else piece
        source = lax.dynamic_update_slice(source, piece, (0, (x - step) % SIDE * (wide // SIDE)))
    mine = jnp.where(first, source[:modes], source[modes:])
    theirs = to_other_core(jnp.where(first, source[modes:], source[:modes]))
    even_source, odd_source = jnp.where(first, mine, theirs), jnp.where(first, theirs, mine)
    odd_source = lax.dynamic_update_slice(jnp.zeros((modes, order), jnp.bfloat16), odd_source, (0, y * wide))

    start = lax.dynamic_slice_in_dim(injected, (CORES * x + core) * modes, modes, 0)
    state = jnp.where(plane == 0, start, jnp.zeros_like(start))
    arrived = [jnp.zeros_like(start)] * SIDE
    onward = lambda z, at: z % 3 == at % 3 and z + 1 < planes
    for at in range(planes):
        odd_part, even_state, state = through_plane(
            at, info, state, arrived, (even_source, odd_source), even, odd
        )
        if at + 1 < planes:
            arrived = [
                send(odd_part, target=lambda z, k, y, x: (z + 1, k, y + turn, x) if onward(z, at) else None)
                for turn in range(SIDE)
            ]

    even_part = lax.dynamic_update_slice(jnp.zeros_like(odd_part), even_state, (0, y * wide))
    mine = jnp.where(first, even_part, odd_part)
    theirs = to_other_core(jnp.where(first, odd_part, even_part))
    both = jnp.concatenate([jnp.where(first, mine, theirs), jnp.where(first, theirs, mine)])
    both = both.reshape(CORES * modes, SIDE * SIDE, -1).transpose(1, 0, 2)
    parts = lax.all_to_all(both, "orb", 0, 0, tiled=True)
    parts = parts.reshape((SIDE, SIDE) + parts.shape[1:]).astype(jnp.float32)
    return parts.sum(0).reshape(1, injected.shape[0], -1).astype(jnp.bfloat16)


def solution(mesh):
    return jax.shard_map(
        on_device,
        mesh=mesh,
        in_specs=(
            P("dom", "orb", None),
            P("dom", "orb", None),
            P("dom", "orb", None),
            P("dom", None, "orb"),
            P(),
        ),
        out_specs=P("dom", None, "orb"),
        check_vma=False,
    )
```

```python
import functools

import jax
import jax.numpy as jnp
from jax import lax
from jax.experimental import pallas as pl
from jax.experimental.pallas import tpu as pltpu
from jax.sharding import PartitionSpec as P

BLOCK = 64
SIDE = 4
CORES = 2
OFFSETS = (0, -1, 1, 2)
WHOLE = pl.BlockSpec(memory_space=pltpu.VMEM)
SCALARS = pl.BlockSpec(memory_space=pltpu.SMEM)


def near(value):
    return pltpu.with_memory_space_constraint(value, pltpu.VMEM)


def far(value):
    return pltpu.with_memory_space_constraint(value, pltpu.HBM)


def bf16(*shape):
    return jax.ShapeDtypeStruct(shape, jnp.bfloat16)


def sent(value, planes, target):
    pairs = []
    for z in range(planes):
        for k in range(CORES):
            for y in range(SIDE):
                for x in range(SIDE):
                    to = target(z, k, y, x)
                    if to is not None:
                        number = lambda z, k, y, x: ((z * CORES + k) * SIDE + y % SIDE) * SIDE + x % SIDE
                        pairs.append((number(z, k, y, x), number(*to)))
    return lax.ppermute(value, ("dom", "orb"), pairs)


def ring(value, move):
    opposite = move(value, 2)
    return [value, move(value, 1), move(value, -1), opposite]


def mask_kernel(info, coupling, pattern, *refs):
    pieces, (masked, done) = refs[:SIDE], refs[SIDE:]
    rows, order = coupling.shape
    fetch = pltpu.make_async_copy(coupling, masked, done)
    fetch.start()
    blocks = order // BLOCK
    column_block = lax.broadcasted_iota(jnp.int32, (blocks, order), 1) // BLOCK
    spread = (column_block == lax.broadcasted_iota(jnp.int32, (blocks, order), 0)).astype(jnp.bfloat16)
    present = jnp.dot(pattern[...].astype(jnp.bfloat16), spread, preferred_element_type=jnp.float32)
    fetch.wait()
    for at in range(rows // BLOCK):
        part = slice(at * BLOCK, (at + 1) * BLOCK)
        masked[part, :] = masked[part, :] * present[at : at + 1, :].astype(jnp.bfloat16)
    wide = order // SIDE
    for offset in range(SIDE):
        turn = lax.rem(info[2] + offset, SIDE)
        pieces[offset][...] = masked[:, pl.ds(pl.multiple_of(turn * wide, wide), wide)]


def masked_pieces(info, coupling, pattern):
    rows, order = coupling.shape
    return pl.pallas_call(
        mask_kernel,
        out_shape=[pltpu.VMEM((rows, order // SIDE), jnp.bfloat16)] * SIDE,
        in_specs=[SCALARS, pl.BlockSpec(memory_space=pltpu.HBM), WHOLE],
        out_specs=[WHOLE] * SIDE,
        scratch_shapes=[pltpu.VMEM((rows, order), jnp.bfloat16), pltpu.SemaphoreType.DMA],
        compiler_params=pltpu.CompilerParams(vmem_limit_bytes=4 << 20),
    )(info, far(coupling), pattern)


def tile_kernel(info, *refs):
    columns, greens = refs[:SIDE], refs[SIDE : 2 * SIDE]
    out, all_columns, all_greens = refs[2 * SIDE + 1 :]
    core, a, b = info[0], info[1], info[2]
    rows = greens[0].shape[0]
    for at, offset in enumerate(OFFSETS):
        row_turn = lax.rem(a + (offset + SIDE), SIDE)
        for inner in range(SIDE):
            turn = lax.rem(b + (SIDE - inner), SIDE)
            block = jnp.where(core == 0, SIDE * row_turn + turn, SIDE * turn + row_turn)
            place = pl.ds(pl.multiple_of(block * rows, rows), rows)
            all_columns[place, :] = columns[at][inner * rows : (inner + 1) * rows, :]
        green_turn = lax.rem(b + (offset + SIDE), SIDE)
        all_greens[pl.ds(pl.multiple_of(green_turn * rows, rows), rows), :] = greens[at][...]
    tile = jnp.dot(all_greens[...], all_columns[...], preferred_element_type=jnp.float32)
    out[...] = tile.T.astype(jnp.bfloat16)


def tiled(info, columns, greens, after):
    wide = columns[0].shape[1]
    order = greens[0].shape[1]
    return pl.pallas_call(
        tile_kernel,
        out_shape=pltpu.VMEM((wide, wide), jnp.bfloat16),
        in_specs=[SCALARS] + [WHOLE] * 8 + [pl.BlockSpec(memory_space=pl.ANY)],
        out_specs=WHOLE,
        scratch_shapes=[pltpu.VMEM((order, wide), jnp.bfloat16), pltpu.VMEM((wide, order), jnp.bfloat16)],
        compiler_params=pltpu.CompilerParams(vmem_limit_bytes=12 << 20),
    )(info, *map(near, columns + greens), after)


def arrange_kernel(offsets, info, *refs):
    count = len(offsets)
    own, other, (even, odd) = refs[:count], refs[count : 2 * count], refs[-2:]
    core, x = info[0], info[3]
    wide = own[0].shape[0]
    block = wide // SIDE

    def arrange(from_even, from_odd):
        for at, offset in enumerate(offsets):
            turn = lax.rem(x + (offset + SIDE), SIDE)
            even[pl.ds(pl.multiple_of(turn * wide, wide), wide), :] = from_even[at][...]
            for row in range(SIDE):
                place = pl.ds(pl.multiple_of((SIDE * row + turn) * block, block), block)
                odd[:, place] = from_odd[at][:, row * block : (row + 1) * block]

    pl.when(core == 0)(lambda: arrange(own, other))
    pl.when(core != 0)(lambda: arrange(other, own))


def arranged(offsets, info, own, other, so_far=()):
    wide = own[0].shape[0]
    order = SIDE * wide
    count = 1 + 2 * len(offsets)
    return pl.pallas_call(
        functools.partial(arrange_kernel, offsets),
        out_shape=[pltpu.VMEM((order, wide), jnp.bfloat16), pltpu.VMEM((wide, order), jnp.bfloat16)],
        in_specs=[SCALARS] + [WHOLE] * (count - 1 + len(so_far)),
        out_specs=[WHOLE] * 2,
        input_output_aliases={count + at: at for at in range(len(so_far))},
        compiler_params=pltpu.CompilerParams(vmem_limit_bytes=4 << 20),
    )(info, *map(near, (*own, *other, *so_far)))


def plane_kernel(at, info, state, *refs):
    arrived, refs = refs[:SIDE], refs[SIDE:]
    even_source, odd_source, even, odd, odd_part, even_state, kept = refs
    plane, y = info[5], info[4]
    wide = even_state.shape[1]
    total = arrived[0][...].astype(jnp.float32)
    for piece in arrived[1:]:
        total += piece[...].astype(jnp.float32)
    total = jnp.where(plane == at, total, 0.0) + state[...].astype(jnp.float32)
    total = total.astype(jnp.bfloat16)
    kept[...] = total
    product = jnp.dot(total, even[...], preferred_element_type=jnp.float32)
    current = (even_source[...].astype(jnp.float32) - product).astype(jnp.bfloat16)
    even_state[...] = current
    product = jnp.dot(current, odd[...], preferred_element_type=jnp.float32)
    odd_part[...] = (odd_source[...].astype(jnp.float32) - product).astype(jnp.bfloat16)


def through_plane(at, info, state, arrived, sources, even, odd):
    modes, order = state.shape
    wide = even.shape[1]
    return pl.pallas_call(
        functools.partial(plane_kernel, at),
        out_shape=[pltpu.VMEM((modes, columns), jnp.bfloat16) for columns in (order, wide, order)],
        in_specs=[SCALARS] + [WHOLE] * 9,
        out_specs=[WHOLE] * 3,
        compiler_params=pltpu.CompilerParams(vmem_limit_bytes=4 << 20),
    )(info, *map(near, (state, *arrived, *sources, even, odd)))


def on_device(green_blocks, couplings, pattern, sources, injected):
    orb, dom = lax.axis_index("orb"), lax.axis_index("dom")
    planes = lax.axis_size("dom") // CORES
    y, x = orb // SIDE, orb % SIDE
    plane, core = dom // CORES, dom % CORES
    first = core == 0
    a, b = jnp.where(first, y, x), jnp.where(first, x, y)
    info = jnp.stack([core, a, b, x, y, plane]).astype(jnp.int32)
    send = functools.partial(sent, planes=planes)
    along_x = lambda value, step: send(value, target=lambda z, k, y, x: (z, k, y, x + step))
    along_b = lambda value, step: send(value, target=lambda z, k, y, x: (z, k, y + k * step, x + (1 - k) * step))
    along_a = lambda value, step: send(value, target=lambda z, k, y, x: (z, k, y + (1 - k) * step, x + k * step))
    to_other_core = lambda value: send(value, target=lambda z, k, y, x: (z, 1 - k, y, x))

    order = injected.shape[1]
    wide = order // SIDE
    modes = injected.shape[0] // (SIDE * CORES)
    mine, theirs = sources[0], to_other_core(sources[0])
    pieces = masked_pieces(info, couplings[0], pattern[0])
    pieces = [pieces[0]] + [along_b(pieces[offset], offset) for offset in range(1, SIDE)]
    green, *_ = lax.optimization_barrier((green_blocks[0], pieces[1]))
    greens = ring(green, along_b)
    columns = ring(jnp.concatenate(pieces), along_a)
    mine, theirs, *_ = lax.optimization_barrier((mine, theirs, columns[1], columns[2]))
    both = jnp.stack([jnp.where(first, mine, theirs), jnp.where(first, theirs, mine)])
    both = both.reshape(CORES, SIDE, CORES, modes, -1)
    by_x = lax.dynamic_index_in_dim(both, core, 2, keepdims=False)
    source = jnp.zeros((CORES * modes, wide), jnp.bfloat16)
    for step in range(SIDE):
        piece = lax.dynamic_index_in_dim(by_x, (x + step) % SIDE, 1, keepdims=False).reshape(CORES * modes, -1)
        piece = along_x(piece, step) if step else piece
        source = lax.dynamic_update_slice(source, piece, (0, (x - step) % SIDE * (wide // SIDE)))
    even_source, odd_source = source[:modes], source[modes:]
    tile = tiled(info, columns, greens, source)
    own = ring(tile, along_x)
    other = [to_other_core(piece) for piece in own]
    even, odd = arranged(OFFSETS[:3], info, own[:3], other[:3])
    even, odd = arranged(OFFSETS[3:], info, own[3:], other[3:], (even, odd))

    odd_source = lax.dynamic_update_slice(jnp.zeros((modes, order), jnp.bfloat16), odd_source, (0, y * wide))

    start = lax.dynamic_slice_in_dim(injected, (CORES * x + core) * modes, modes, 0)
    state = jnp.where(plane == 0, start, jnp.zeros_like(start))
    arrived = [jnp.zeros_like(start)] * SIDE
    onward = lambda z, at: z % 3 == at % 3 and z + 1 < planes
    for at in range(planes):
        odd_part, even_state, state = through_plane(
            at, info, state, arrived, (even_source, odd_source), even, odd
        )
        if at + 1 < planes:
            arrived = [
                send(odd_part, target=lambda z, k, y, x: (z + 1, k, y + turn, x) if onward(z, at) else None)
                for turn in (2, 1, 3, 0)
            ]

    even_part = lax.dynamic_update_slice(jnp.zeros_like(odd_part), even_state, (0, y * wide))
    mine = jnp.where(first, even_part, odd_part)
    theirs = to_other_core(jnp.where(first, odd_part, even_part))
    both = jnp.concatenate([jnp.where(first, mine, theirs), jnp.where(first, theirs, mine)])
    both = both.reshape(CORES * modes, SIDE * SIDE, -1).transpose(1, 0, 2)
    parts = lax.all_to_all(both, "orb", 0, 0, tiled=True)
    parts = parts.reshape((SIDE, SIDE) + parts.shape[1:]).astype(jnp.float32)
    return parts.sum(0).reshape(1, injected.shape[0], -1).astype(jnp.bfloat16)


def solution(mesh):
    return jax.shard_map(
        on_device,
        mesh=mesh,
        in_specs=(
            P("dom", "orb", None),
            P("dom", "orb", None),
            P("dom", "orb", None),
            P("dom", None, "orb"),
            P(),
        ),
        out_specs=P("dom", None, "orb"),
        check_vma=False,
    )
```

```python
import functools

import jax
import jax.numpy as jnp
from jax import lax
from jax.experimental import pallas as pl
from jax.experimental.pallas import tpu as pltpu
from jax.sharding import PartitionSpec as P

BLOCK = 64
SIDE = 4
CORES = 2
OFFSETS = (0, -1, 1, 2)
WHOLE = pl.BlockSpec(memory_space=pltpu.VMEM)


def near(value):
    return pltpu.with_memory_space_constraint(value, pltpu.VMEM)


def far(value):
    return pltpu.with_memory_space_constraint(value, pltpu.HBM)


def bf16(*shape):
    return jax.ShapeDtypeStruct(shape, jnp.bfloat16)


def position():
    core, orb = lax.rem(lax.axis_index("dom"), CORES), lax.axis_index("orb")
    y, x = lax.div(orb, SIDE), lax.rem(orb, SIDE)
    return core, jnp.where(core == 0, y, x), jnp.where(core == 0, x, y), x, y


def sent(value, planes, target):
    pairs = []
    for z in range(planes):
        for k in range(CORES):
            for y in range(SIDE):
                for x in range(SIDE):
                    to = target(z, k, y, x)
                    if to is not None:
                        number = lambda z, k, y, x: ((z * CORES + k) * SIDE + y % SIDE) * SIDE + x % SIDE
                        pairs.append((number(z, k, y, x), number(*to)))
    return lax.ppermute(value, ("dom", "orb"), pairs)


def ring(value, move):
    opposite = move(value, 2)
    return [value, move(value, 1), move(value, -1), opposite]


def mask_kernel(coupling, pattern, *refs):
    pieces, (masked, done) = refs[:SIDE], refs[SIDE:]
    rows, order = coupling.shape
    fetch = pltpu.make_async_copy(coupling, masked, done)
    fetch.start()
    blocks = order // BLOCK
    column_block = lax.broadcasted_iota(jnp.int32, (blocks, order), 1) // BLOCK
    spread = (column_block == lax.broadcasted_iota(jnp.int32, (blocks, order), 0)).astype(jnp.bfloat16)
    present = jnp.dot(pattern[...].astype(jnp.bfloat16), spread, preferred_element_type=jnp.float32)
    fetch.wait()
    for at in range(rows // BLOCK):
        part = slice(at * BLOCK, (at + 1) * BLOCK)
        masked[part, :] = masked[part, :] * present[at : at + 1, :].astype(jnp.bfloat16)
    wide = order // SIDE
    for offset in range(SIDE):
        turn = lax.rem(position()[2] + offset, SIDE)
        pieces[offset][...] = masked[:, pl.ds(pl.multiple_of(turn * wide, wide), wide)]


def masked_pieces(coupling, pattern):
    rows, order = coupling.shape
    return pl.pallas_call(
        mask_kernel,
        out_shape=[pltpu.VMEM((rows, order // SIDE), jnp.bfloat16)] * SIDE,
        in_specs=[pl.BlockSpec(memory_space=pltpu.HBM), WHOLE],
        out_specs=[WHOLE] * SIDE,
        scratch_shapes=[pltpu.VMEM((rows, order), jnp.bfloat16), pltpu.SemaphoreType.DMA],
        compiler_params=pltpu.CompilerParams(vmem_limit_bytes=4 << 20),
    )(far(coupling), pattern)


def tile_kernel(*refs):
    columns, greens = refs[:SIDE], refs[SIDE : 2 * SIDE]
    out, all_columns, all_greens = refs[-3:]
    core, a, b, _, _ = position()
    rows = greens[0].shape[0]
    for at, offset in enumerate(OFFSETS):
        row_turn = lax.rem(a + (offset + SIDE), SIDE)
        for inner in range(SIDE):
            turn = lax.rem(b + (SIDE - inner), SIDE)
            block = jnp.where(core == 0, SIDE * row_turn + turn, SIDE * turn + row_turn)
            place = pl.ds(pl.multiple_of(block * rows, rows), rows)
            all_columns[place, :] = columns[at][inner * rows : (inner + 1) * rows, :]
        green_turn = lax.rem(b + (offset + SIDE), SIDE)
        all_greens[pl.ds(pl.multiple_of(green_turn * rows, rows), rows), :] = greens[at][...]
    tile = jnp.dot(all_greens[...], all_columns[...], preferred_element_type=jnp.float32)
    out[...] = tile.T.astype(jnp.bfloat16)


def tiled(columns, greens, after):
    wide = columns[0].shape[1]
    order = greens[0].shape[1]
    return pl.pallas_call(
        tile_kernel,
        out_shape=pltpu.VMEM((wide, wide), jnp.bfloat16),
        in_specs=[WHOLE] * 8 + [pl.BlockSpec(memory_space=pl.ANY)] * len(after),
        out_specs=WHOLE,
        scratch_shapes=[pltpu.VMEM((order, wide), jnp.bfloat16), pltpu.VMEM((wide, order), jnp.bfloat16)],
        compiler_params=pltpu.CompilerParams(vmem_limit_bytes=12 << 20),
    )(*map(near, columns + greens), *after)


def arrange_kernel(offsets, *refs):
    count = len(offsets)
    own, other, (even, odd) = refs[:count], refs[count : 2 * count], refs[-2:]
    core, _, _, x, _ = position()
    wide = own[0].shape[0]
    block = wide // SIDE

    def arrange(from_even, from_odd):
        for at, offset in enumerate(offsets):
            turn = lax.rem(x + (offset + SIDE), SIDE)
            even[pl.ds(pl.multiple_of(turn * wide, wide), wide), :] = from_even[at][...]
            for row in range(SIDE):
                place = pl.ds(pl.multiple_of((SIDE * row + turn) * block, block), block)
                odd[:, place] = from_odd[at][:, row * block : (row + 1) * block]

    pl.when(core == 0)(lambda: arrange(own, other))
    pl.when(core != 0)(lambda: arrange(other, own))


def arranged(offsets, own, other, so_far=()):
    wide = own[0].shape[0]
    order = SIDE * wide
    count = 2 * len(offsets)
    return pl.pallas_call(
        functools.partial(arrange_kernel, offsets),
        out_shape=[pltpu.VMEM((order, wide), jnp.bfloat16), pltpu.VMEM((wide, order), jnp.bfloat16)],
        in_specs=[WHOLE] * (count + len(so_far)),
        out_specs=[WHOLE] * 2,
        input_output_aliases={count + at: at for at in range(len(so_far))},
        compiler_params=pltpu.CompilerParams(vmem_limit_bytes=4 << 20),
    )(*map(near, (*own, *other, *so_far)))


def plane_kernel(at, due, state, *refs):
    arrived, refs = refs[:SIDE], refs[SIDE:]
    even_source, odd_source, even, odd, odd_part, even_state, kept = refs
    total = arrived[0][...].astype(jnp.float32)
    for piece in arrived[1:]:
        total += piece[...].astype(jnp.float32)
    total = jnp.where(due[at : at + 1, :1] > 0, total, 0.0) + state[...].astype(jnp.float32)
    total = total.astype(jnp.bfloat16)
    kept[...] = total
    product = jnp.dot(total, even[...], preferred_element_type=jnp.float32)
    current = (even_source[...].astype(jnp.float32) - product).astype(jnp.bfloat16)
    even_state[...] = current
    product = jnp.dot(current, odd[...], preferred_element_type=jnp.float32)
    odd_part[...] = (odd_source[...].astype(jnp.float32) - product).astype(jnp.bfloat16)


def through_plane(at, due, state, arrived, sources, even, odd):
    modes, order = state.shape
    wide = even.shape[1]
    return pl.pallas_call(
        functools.partial(plane_kernel, at),
        out_shape=[pltpu.VMEM((modes, columns), jnp.bfloat16) for columns in (order, wide, order)],
        in_specs=[WHOLE] * 10,
        out_specs=[WHOLE] * 3,
        compiler_params=pltpu.CompilerParams(vmem_limit_bytes=4 << 20),
    )(*map(near, (due, state, *arrived, *sources, even, odd)))


def on_device(green_blocks, couplings, pattern, sources, injected):
    orb, dom = lax.axis_index("orb"), lax.axis_index("dom")
    planes = lax.axis_size("dom") // CORES
    y, x = orb // SIDE, orb % SIDE
    plane, core = dom // CORES, dom % CORES
    first = core == 0
    send = functools.partial(sent, planes=planes)
    along_x = lambda value, step: send(value, target=lambda z, k, y, x: (z, k, y, x + step))
    along_b = lambda value, step: send(value, target=lambda z, k, y, x: (z, k, y + k * step, x + (1 - k) * step))
    along_a = lambda value, step: send(value, target=lambda z, k, y, x: (z, k, y + (1 - k) * step, x + k * step))
    to_other_core = lambda value: send(value, target=lambda z, k, y, x: (z, 1 - k, y, x))

    order = injected.shape[1]
    wide = order // SIDE
    modes = injected.shape[0] // (SIDE * CORES)
    mine, theirs = sources[0], to_other_core(sources[0])
    pieces = masked_pieces(couplings[0], pattern[0])
    pieces = [pieces[0]] + [along_b(pieces[offset], offset) for offset in range(1, SIDE)]
    green, *_ = lax.optimization_barrier((green_blocks[0], pieces[1]))
    greens = ring(green, along_b)
    columns = ring(jnp.concatenate(pieces), along_a)
    mine, theirs, *_ = lax.optimization_barrier((mine, theirs, columns[1], columns[2]))
    both = jnp.stack([jnp.where(first, mine, theirs), jnp.where(first, theirs, mine)])
    both = both.reshape(CORES, SIDE, CORES, modes, -1)
    by_x = lax.dynamic_index_in_dim(both, core, 2, keepdims=False)
    source = jnp.zeros((CORES * modes, wide), jnp.bfloat16)
    for step in range(SIDE):
        piece = lax.dynamic_index_in_dim(by_x, (x + step) % SIDE, 1, keepdims=False).reshape(CORES * modes, -1)
        piece = along_x(piece, step) if step else piece
        source = lax.dynamic_update_slice(source, piece, (0, (x - step) % SIDE * (wide // SIDE)))
    even_source, odd_source = source[:modes], source[modes:]
    start = lax.dynamic_slice_in_dim(injected, (CORES * x + core) * modes, modes, 0)
    state = jnp.where(plane == 0, start, jnp.zeros_like(start))
    due = jnp.where(jnp.arange(planes)[:, None] == plane, jnp.ones((planes, 128), jnp.float32), 0.0)
    tile = tiled(columns, greens, (source, state, due))
    own = ring(tile, along_x)
    other = [to_other_core(piece) for piece in own]
    even, odd = arranged(OFFSETS[:3], own[:3], other[:3])
    even, odd = arranged(OFFSETS[3:], own[3:], other[3:], (even, odd))

    odd_source = lax.dynamic_update_slice(jnp.zeros((modes, order), jnp.bfloat16), odd_source, (0, y * wide))

    arrived = [jnp.zeros_like(start)] * SIDE
    onward = lambda z, at: z % 3 == at % 3 and z + 1 < planes
    for at in range(planes):
        odd_part, even_state, state = through_plane(
            at, due, state, arrived, (even_source, odd_source), even, odd
        )
        if at + 1 < planes:
            arrived = [
                send(odd_part, target=lambda z, k, y, x: (z + 1, k, y + turn, x) if onward(z, at) else None)
                for turn in (2, 1, 3, 0)
            ]

    even_part = lax.dynamic_update_slice(jnp.zeros_like(odd_part), even_state, (0, y * wide))
    mine = jnp.where(first, even_part, odd_part)
    theirs = to_other_core(jnp.where(first, odd_part, even_part))
    both = jnp.concatenate([jnp.where(first, mine, theirs), jnp.where(first, theirs, mine)])
    both = both.reshape(CORES * modes, SIDE * SIDE, -1).transpose(1, 0, 2)
    parts = lax.all_to_all(both, "orb", 0, 0, tiled=True)
    parts = parts.reshape((SIDE, SIDE) + parts.shape[1:]).astype(jnp.float32)
    return parts.sum(0).reshape(1, injected.shape[0], -1).astype(jnp.bfloat16)


def solution(mesh):
    return jax.shard_map(
        on_device,
        mesh=mesh,
        in_specs=(
            P("dom", "orb", None),
            P("dom", "orb", None),
            P("dom", "orb", None),
            P("dom", None, "orb"),
            P(),
        ),
        out_specs=P("dom", None, "orb"),
        check_vma=False,
    )
```

```python
import functools

import jax
import jax.numpy as jnp
from jax import lax
from jax.experimental import pallas as pl
from jax.experimental.pallas import tpu as pltpu
from jax.sharding import PartitionSpec as P

BLOCK = 64
SIDE = 4
CORES = 2
OFFSETS = (0, -1, 1, 2)
WHOLE = pl.BlockSpec(memory_space=pltpu.VMEM)


def near(value):
    return pltpu.with_memory_space_constraint(value, pltpu.VMEM)


def far(value):
    return pltpu.with_memory_space_constraint(value, pltpu.HBM)


def bf16(*shape):
    return jax.ShapeDtypeStruct(shape, jnp.bfloat16)


def position():
    core, orb = lax.rem(lax.axis_index("dom"), CORES), lax.axis_index("orb")
    y, x = lax.div(orb, SIDE), lax.rem(orb, SIDE)
    return core, jnp.where(core == 0, y, x), jnp.where(core == 0, x, y), x, y


def sent(value, planes, target):
    pairs = []
    for z in range(planes):
        for k in range(CORES):
            for y in range(SIDE):
                for x in range(SIDE):
                    to = target(z, k, y, x)
                    if to is not None:
                        number = lambda z, k, y, x: ((z * CORES + k) * SIDE + y % SIDE) * SIDE + x % SIDE
                        pairs.append((number(z, k, y, x), number(*to)))
    return lax.ppermute(value, ("dom", "orb"), pairs)


def ring(value, move):
    opposite = move(value, 2)
    return [value, move(value, 1), move(value, -1), opposite]


def mask_kernel(coupling, pattern, *refs):
    pieces, (masked, present_blocks, done) = refs[:SIDE], refs[SIDE:]
    rows, order = coupling.shape
    fetch_blocks = pltpu.make_async_copy(pattern, present_blocks, done.at[1])
    fetch_blocks.start()
    fetch = pltpu.make_async_copy(coupling, masked, done.at[0])
    fetch.start()
    blocks = order // BLOCK
    column_block = lax.broadcasted_iota(jnp.int32, (blocks, order), 1) // BLOCK
    spread = (column_block == lax.broadcasted_iota(jnp.int32, (blocks, order), 0)).astype(jnp.bfloat16)
    fetch_blocks.wait()
    present = jnp.dot(present_blocks[...].astype(jnp.bfloat16), spread, preferred_element_type=jnp.float32)
    fetch.wait()
    for at in range(rows // BLOCK):
        part = slice(at * BLOCK, (at + 1) * BLOCK)
        masked[part, :] = masked[part, :] * present[at : at + 1, :].astype(jnp.bfloat16)
    wide = order // SIDE
    for offset in range(SIDE):
        turn = lax.rem(position()[2] + offset, SIDE)
        pieces[offset][...] = masked[:, pl.ds(pl.multiple_of(turn * wide, wide), wide)]


def masked_pieces(coupling, pattern):
    rows, order = coupling.shape
    return pl.pallas_call(
        mask_kernel,
        out_shape=[pltpu.VMEM((rows, order // SIDE), jnp.bfloat16)] * SIDE,
        in_specs=[pl.BlockSpec(memory_space=pltpu.HBM)] * 2,
        out_specs=[WHOLE] * SIDE,
        scratch_shapes=[
            pltpu.VMEM((rows, order), jnp.bfloat16),
            pltpu.VMEM(pattern.shape, jnp.int32),
            pltpu.SemaphoreType.DMA((2,)),
        ],
        compiler_params=pltpu.CompilerParams(vmem_limit_bytes=4 << 20),
    )(far(coupling), far(pattern))


def tile_kernel(*refs):
    columns, greens = refs[:SIDE], refs[SIDE : 2 * SIDE]
    out, all_columns, all_greens = refs[-3:]
    core, a, b, _, _ = position()
    rows = greens[0].shape[0]
    for at, offset in enumerate(OFFSETS):
        row_turn = lax.rem(a + (offset + SIDE), SIDE)
        for inner in range(SIDE):
            turn = lax.rem(b + (SIDE - inner), SIDE)
            block = jnp.where(core == 0, SIDE * row_turn + turn, SIDE * turn + row_turn)
            place = pl.ds(pl.multiple_of(block * rows, rows), rows)
            all_columns[place, :] = columns[at][inner * rows : (inner + 1) * rows, :]
        green_turn = lax.rem(b + (offset + SIDE), SIDE)
        all_greens[pl.ds(pl.multiple_of(green_turn * rows, rows), rows), :] = greens[at][...]
    tile = jnp.dot(all_greens[...], all_columns[...], preferred_element_type=jnp.float32)
    out[...] = tile.T.astype(jnp.bfloat16)


def tiled(columns, greens, after):
    wide = columns[0].shape[1]
    order = greens[0].shape[1]
    return pl.pallas_call(
        tile_kernel,
        out_shape=pltpu.VMEM((wide, wide), jnp.bfloat16),
        in_specs=[WHOLE] * 8 + [pl.BlockSpec(memory_space=pl.ANY)] * len(after),
        out_specs=WHOLE,
        scratch_shapes=[pltpu.VMEM((order, wide), jnp.bfloat16), pltpu.VMEM((wide, order), jnp.bfloat16)],
        compiler_params=pltpu.CompilerParams(vmem_limit_bytes=12 << 20),
    )(*map(near, columns + greens), *after)


def arrange_kernel(offsets, *refs):
    count = len(offsets)
    own, other, (even, odd) = refs[:count], refs[count : 2 * count], refs[-2:]
    core, _, _, x, _ = position()
    wide = own[0].shape[0]
    block = wide // SIDE

    def arrange(from_even, from_odd):
        for at, offset in enumerate(offsets):
            turn = lax.rem(x + (offset + SIDE), SIDE)
            even[pl.ds(pl.multiple_of(turn * wide, wide), wide), :] = from_even[at][...]
            for row in range(SIDE):
                place = pl.ds(pl.multiple_of((SIDE * row + turn) * block, block), block)
                odd[:, place] = from_odd[at][:, row * block : (row + 1) * block]

    pl.when(core == 0)(lambda: arrange(own, other))
    pl.when(core != 0)(lambda: arrange(other, own))


def arranged(offsets, own, other, so_far=()):
    wide = own[0].shape[0]
    order = SIDE * wide
    count = 2 * len(offsets)
    return pl.pallas_call(
        functools.partial(arrange_kernel, offsets),
        out_shape=[pltpu.VMEM((order, wide), jnp.bfloat16), pltpu.VMEM((wide, order), jnp.bfloat16)],
        in_specs=[WHOLE] * (count + len(so_far)),
        out_specs=[WHOLE] * 2,
        input_output_aliases={count + at: at for at in range(len(so_far))},
        compiler_params=pltpu.CompilerParams(vmem_limit_bytes=4 << 20),
    )(*map(near, (*own, *other, *so_far)))


def plane_kernel(at, due, state, *refs):
    arrived, refs = refs[:SIDE], refs[SIDE:]
    even_source, odd_source, even, odd, odd_part, even_state, kept = refs
    total = arrived[0][...].astype(jnp.float32)
    for piece in arrived[1:]:
        total += piece[...].astype(jnp.float32)
    total = jnp.where(due[at : at + 1, :1] > 0, total, 0.0) + state[...].astype(jnp.float32)
    total = total.astype(jnp.bfloat16)
    kept[...] = total
    product = jnp.dot(total, even[...], preferred_element_type=jnp.float32)
    current = (even_source[...].astype(jnp.float32) - product).astype(jnp.bfloat16)
    even_state[...] = current
    product = jnp.dot(current, odd[...], preferred_element_type=jnp.float32)
    odd_part[...] = (odd_source[...].astype(jnp.float32) - product).astype(jnp.bfloat16)


def through_plane(at, due, state, arrived, sources, even, odd):
    modes, order = state.shape
    wide = even.shape[1]
    return pl.pallas_call(
        functools.partial(plane_kernel, at),
        out_shape=[pltpu.VMEM((modes, columns), jnp.bfloat16) for columns in (order, wide, order)],
        in_specs=[WHOLE] * 10,
        out_specs=[WHOLE] * 3,
        compiler_params=pltpu.CompilerParams(vmem_limit_bytes=4 << 20),
    )(*map(near, (due, state, *arrived, *sources, even, odd)))


def on_device(green_blocks, couplings, pattern, sources, injected):
    orb, dom = lax.axis_index("orb"), lax.axis_index("dom")
    planes = lax.axis_size("dom") // CORES
    y, x = orb // SIDE, orb % SIDE
    plane, core = dom // CORES, dom % CORES
    first = core == 0
    send = functools.partial(sent, planes=planes)
    along_x = lambda value, step: send(value, target=lambda z, k, y, x: (z, k, y, x + step))
    along_b = lambda value, step: send(value, target=lambda z, k, y, x: (z, k, y + k * step, x + (1 - k) * step))
    along_a = lambda value, step: send(value, target=lambda z, k, y, x: (z, k, y + (1 - k) * step, x + k * step))
    to_other_core = lambda value: send(value, target=lambda z, k, y, x: (z, 1 - k, y, x))

    order = injected.shape[1]
    wide = order // SIDE
    modes = injected.shape[0] // (SIDE * CORES)
    mine, theirs = sources[0], to_other_core(sources[0])
    pieces = masked_pieces(couplings[0], pattern[0])
    pieces = [pieces[0]] + [along_b(pieces[offset], offset) for offset in range(1, SIDE)]
    green, *_ = lax.optimization_barrier((green_blocks[0], pieces[1]))
    greens = ring(green, along_b)
    columns = ring(jnp.concatenate(pieces), along_a)
    mine, theirs, *_ = lax.optimization_barrier((mine, theirs, columns[1], columns[2]))
    both = jnp.stack([jnp.where(first, mine, theirs), jnp.where(first, theirs, mine)])
    both = both.reshape(CORES, SIDE, CORES, modes, -1)
    by_x = lax.dynamic_index_in_dim(both, core, 2, keepdims=False)
    source = jnp.zeros((CORES * modes, wide), jnp.bfloat16)
    for step in range(SIDE):
        piece = lax.dynamic_index_in_dim(by_x, (x + step) % SIDE, 1, keepdims=False).reshape(CORES * modes, -1)
        piece = along_x(piece, step) if step else piece
        source = lax.dynamic_update_slice(source, piece, (0, (x - step) % SIDE * (wide // SIDE)))
    even_source, odd_source = source[:modes], source[modes:]
    start = lax.dynamic_slice_in_dim(injected, (CORES * x + core) * modes, modes, 0)
    state = jnp.where(plane == 0, start, jnp.zeros_like(start))
    due = jnp.where(jnp.arange(planes)[:, None] == plane, jnp.ones((planes, 128), jnp.float32), 0.0)
    tile = tiled(columns, greens, (source, state, due))
    own = ring(tile, along_x)
    other = [to_other_core(piece) for piece in own]
    even, odd = arranged(OFFSETS[:3], own[:3], other[:3])
    even, odd = arranged(OFFSETS[3:], own[3:], other[3:], (even, odd))

    odd_source = lax.dynamic_update_slice(jnp.zeros((modes, order), jnp.bfloat16), odd_source, (0, y * wide))

    arrived = [jnp.zeros_like(start)] * SIDE
    onward = lambda z, at: z % 3 == at % 3 and z + 1 < planes
    for at in range(planes):
        odd_part, even_state, state = through_plane(
            at, due, state, arrived, (even_source, odd_source), even, odd
        )
        if at + 1 < planes:
            arrived = [
                send(odd_part, target=lambda z, k, y, x: (z + 1, k, y + turn, x) if onward(z, at) else None)
                for turn in (2, 1, 3, 0)
            ]

    even_part = lax.dynamic_update_slice(jnp.zeros_like(odd_part), even_state, (0, y * wide))
    mine = jnp.where(first, even_part, odd_part)
    theirs = to_other_core(jnp.where(first, odd_part, even_part))
    both = jnp.concatenate([jnp.where(first, mine, theirs), jnp.where(first, theirs, mine)])
    both = both.reshape(CORES * modes, SIDE * SIDE, -1).transpose(1, 0, 2)
    parts = lax.all_to_all(both, "orb", 0, 0, tiled=True)
    parts = parts.reshape((SIDE, SIDE) + parts.shape[1:]).astype(jnp.float32)
    return parts.sum(0).reshape(1, injected.shape[0], -1).astype(jnp.bfloat16)


def solution(mesh):
    return jax.shard_map(
        on_device,
        mesh=mesh,
        in_specs=(
            P("dom", "orb", None),
            P("dom", "orb", None),
            P("dom", "orb", None),
            P("dom", None, "orb"),
            P(),
        ),
        out_specs=P("dom", None, "orb"),
        check_vma=False,
    )
```
